128 devices in a mesh: ctx: 16 (over z_hi, y, core), head: 8 (over x, z_lo).
Axes of the slice: x: 4, y: 4, z: 4 (z_hi: 2, z_lo: 2; z = z_hi * 2 + z_lo), core: 2. Of those that a mesh axis runs over, the one named last changes fastest.
Arguments:
- queries: bfloat16 [3072, 128, 576], P('ctx', 'head'), may hold values from -38 to 38
- latent_kv: bfloat16 [3072, 576], P('ctx'), may hold values from -4.2 to 4.2
- doc_ids: int32 [3072], P('ctx'), may hold values from 0 to 3, never falling along the last dimension, each value on 1 to 1536 neighbouring positions
- w_uv: bfloat16 [128, 512, 128], P('head'), may hold values from -1.25 to 1.25
- w_o: bfloat16 [16384, 4096], P('head'), may hold values from -0.625 to 0.625
Outputs:
- attended: bfloat16 [3072, 4096], P('ctx', 'head')
The draws below stay inside these ranges and needn't reach their ends.
Inputs may be any that keep to these rules, and one draw needn't show every extreme that they name: `doc_ids`: document ids never fall along the prompt.
All inputs are finite; a program needn't handle non-finite values.
Results may differ from the reference program's by a relative error of at most 0.019.
Values may be sent and summed in bfloat16 or wider, within the bound.
No kernel may reach another device: no remote copies, remote signals or barrier semaphores. Data moves between devices by JAX's collectives and lax.ppermute only.
A program may use at most 192 MiB of HBM per device.

```python
import math
import jax
import jax.numpy as jnp
import numpy as np
from jax import lax

H = 128
C = 512
VH = 128
DOUT = 4096
KW = 576
TOKENS = 3072


def shared_keys(key, spread):
    base = jnp.clip(jax.random.normal(key, (TOKENS, KW), jnp.float32), -3.5, 3.5)
    factor = 1.0 + spread * jax.random.uniform(jax.random.fold_in(key, 7), (TOKENS, KW), jnp.float32)
    return base * factor


def draw_latent_kv(key, part):
    spread = 0.0
    keys_drawn = shared_keys(key, spread)
    return keys_drawn.astype(jnp.bfloat16)


def draw_queries(key, part):
    key = jax.random.fold_in(key, 2)
    noise = jnp.clip(jax.random.normal(key, (TOKENS, H, KW), jnp.float32), -3.5, 3.5)
    return noise.astype(jnp.bfloat16)


def spiked(result, stream_key, source, target, blocks, factor):
    owner, partner = [(jnp.arange(result.shape[axis_at]) // (result.shape[axis_at] // blocks)).reshape([-1 if axis == axis_at else 1 for axis in range(result.ndim)]) for axis_at in (source, target)]
    chosen = jax.random.permutation(stream_key, blocks)[partner]
    strong = (owner == chosen) | (owner == (partner + blocks // 2) % blocks)
    return jnp.where(strong, factor * result, result)


def shard_levels(stream_key, dims, cuts, least, largest):
    def one(axis_at, parts):
        steps = jax.random.uniform(jax.random.fold_in(jax.random.fold_in(stream_key, 6), axis_at), (parts,), jnp.float32, least / len(cuts), largest / len(cuts))
        return jnp.repeat(jnp.exp(steps), dims[axis_at] // parts).reshape((-1,) + (1,) * (len(dims) - axis_at - 1))

    factor_of = one(*cuts[0])
    for cut in cuts[1:]:
        factor_of = factor_of * one(*cut)
    return factor_of


def length_profile(number_of, total, bound, slope):
    weights = [(1 << 20) // math.isqrt(rank ** slope) + 1 for rank in range(2, number_of + 1)]
    surplus, given = total - bound - (number_of - 1), [1] * (number_of - 1)
    while surplus > 0:
        candidates = [i for i in range(number_of - 1) if given[i] < bound]
        whole, remaining = sum([weights[i] for i in candidates]), surplus
        for i in candidates:
            extra = min(bound - given[i], max(1, remaining * weights[i] // whole), surplus)
            given[i] = given[i] + extra
            surplus = surplus - extra
    return np.array([bound] + given)


def uneven(own_key, amount, total, reach, lean):
    if amount == 2:
        one = jax.random.randint(own_key, (), max(1, total - reach), min(reach, total - 1) + 1)
        return jnp.stack([one, total - one])
    sizes = jnp.asarray(length_profile(amount, total, reach, lean), jnp.int32)
    pairs = (amount - 1) // 2
    source_of, taker = sizes[1:1 + 2 * pairs:2], sizes[2:2 + 2 * pairs:2]
    margin = jnp.minimum(source_of - 1, reach - taker)
    shifted = jax.random.randint(jax.random.fold_in(own_key, 1), (pairs,), 0, 1 << 20) % (margin + 1)
    sizes = sizes.at[1:1 + 2 * pairs:2].set(source_of - shifted).at[2:2 + 2 * pairs:2].set(taker + shifted)
    return sizes[jax.random.permutation(jax.random.fold_in(own_key, 2), amount)]


def normal_values(stream_key, dims, scale, reach, shards=(), kind=jnp.bfloat16):
    entries = jax.random.normal(stream_key, dims, jnp.float32) * scale
    if len(shards) > 0:
        entries = shard_levels(stream_key, dims, shards, -0.22, 0.18) * entries
    return jnp.clip(entries, min=-reach, max=reach).astype(kind)


def bell_draw_with(key, dims, deviation, bound, shards, heavy, kind=jnp.bfloat16):
    result = deviation * jax.random.normal(key, dims, jnp.float32)
    if shards:
        result = result * shard_levels(key, dims, shards, -0.22, 0.18)
    return jnp.clip(spiked(result, jax.random.fold_in(key, 3), *heavy), -bound, bound).astype(kind)


def setup_inputs(seed: int = 0) -> dict:
    splits = jax.random.split(jax.random.key(seed), 6)
    return {
        "queries": draw_queries(jax.random.fold_in(splits[5], 71), 0),
        "latent_kv": draw_latent_kv(jax.random.fold_in(splits[5], 71), 0),
        "doc_ids": jnp.searchsorted(jnp.cumsum(uneven(splits[2], 4, TOKENS, TOKENS // 2, 2)), jnp.arange(TOKENS), side="right").astype(jnp.int32),
        "w_uv": normal_values(splits[3], (H, C, VH), (2.0 / C ** 0.5), 1.25, ((0, 8),)),
        "w_o": bell_draw_with(splits[4], (H * VH, DOUT), (4.0 / (H * VH) ** 0.5), 0.625, ((0, 8),), (0, 1, 8, 2.0)),
    }


score_scale = 0.07216878


def reference(queries, latent_kv, doc_ids, w_uv, w_o):
    positions = jnp.arange(TOKENS, dtype=jnp.int32)
    visible = (positions[None, :] <= positions[:, None]) & (doc_ids[None, :] == doc_ids[:, None])
    keys_full = latent_kv.astype(jnp.float32)
    values_full = keys_full[:, :C]
    group = 8
    grouped = queries.reshape(TOKENS, H // group, group, KW).transpose(1, 0, 2, 3)

    def per_group(query_group):
        scores = jnp.einsum("tgk,jk->tgj", query_group.astype(jnp.float32), keys_full) * score_scale
        scores = jnp.where(visible[:, None, :], scores, -1e30)
        top = jnp.max(scores, axis=-1)
        expd = jnp.where(visible[:, None, :], jnp.exp(scores - top[..., None]), 0.0)
        total = jnp.sum(expd, axis=-1)
        rounded = lax.optimization_barrier(expd.astype(jnp.bfloat16)).astype(jnp.float32)
        summed = jnp.einsum("tgj,jc->tgc", rounded, values_full)
        return (summed / total[..., None]).astype(jnp.bfloat16)

    latent_out = lax.map(per_group, grouped).transpose(1, 0, 2, 3).reshape(TOKENS, H, C)
    head_out = jnp.einsum("thc,hcd->thd", latent_out.astype(jnp.float32), w_uv.astype(jnp.float32)).astype(jnp.bfloat16)
    flat = head_out.reshape(TOKENS, H * VH)
    return jnp.dot(flat, w_o, preferred_element_type=jnp.float32).astype(jnp.bfloat16)
```

```python
import functools

import jax
import jax.numpy as jnp
from jax import lax
from jax.experimental import pallas as pl
from jax.experimental.pallas import tpu as pltpu
from jax.sharding import PartitionSpec as P

score_scale = 0.07216878
log2e = 1.4426950408889634
tok, heads, width, latent, vdim = 192, 16, 576, 512, 128
wide = 640
back = 8
window = 1792
own_at = back * tok
group = 2 * tok
groups = heads * tok // group
big = 2.0**100
peers = 8
columns = 512


def attend(
    info, q_hbm, own, r1, r2, r3, r4, m0, m1, m2, m3, m4, wuv_hbm, wo_hbm, *rest
):
    outs = rest[:peers]
    keys, q, wuv, wo, s_a, s_b, p_a, p_b, bias, lat, ho, key_sem, q_sem, w_sem, wo_sem = rest[peers:]
    core, me = info[0], info[1]

    def key_copy(src, block):
        return pltpu.make_async_copy(src, keys.at[pl.ds(block * tok, tok)], key_sem.at[block])

    for block, src in ((0, r4), (2, r3), (4, r2), (6, r1), (8, own)):
        key_copy(src, block).start()

    @pl.when(core == 0)
    def _():
        for block, src in ((1, m4), (3, m3), (5, m2), (7, m1)):
            key_copy(src, block).start()

    @pl.when(core != 0)
    def _():
        for block, src in ((1, m3), (3, m2), (5, m1), (7, m0)):
            key_copy(src, block).start()

    def q_copy(i):
        return pltpu.make_async_copy(
            q_hbm.at[pl.ds(i * group, group)], q.at[pl.ds(i * group, group)], q_sem.at[i]
        )

    def wo_copy(k):
        at = pl.multiple_of((me ^ k) * columns, columns)
        return pltpu.make_async_copy(wo_hbm.at[:, pl.ds(at, columns)], wo.at[k], wo_sem.at[k])

    for i in range(groups):
        q_copy(i).start()
    wuv_copy = pltpu.make_async_copy(wuv_hbm, wuv, w_sem)
    wuv_copy.start()
    for k in range(peers):
        wo_copy(k).start()

    keys[pl.ds(9 * tok, window - 9 * tok), :] = jnp.zeros((window - 9 * tok, wide), jnp.bfloat16)
    bias[...] = jnp.where(
        lax.broadcasted_iota(jnp.int32, (tok, 256), 1) <= lax.broadcasted_iota(jnp.int32, (tok, 256), 0),
        0.0,
        -big,
    )
    for block in range(9):
        key_copy(own, block).wait()

    def scores(i, s):
        rows = q[pl.ds(pl.multiple_of(i * group, group), group), :]
        for j in range(window // 256):
            part = lax.dot_general(
                rows,
                keys[j * 256 : (j + 1) * 256, :],
                (((1,), (1,)), ((), ())),
                preferred_element_type=jnp.float32,
            )
            if j == own_at // 256:
                part = part + jnp.concatenate([bias[...], bias[...]], axis=0)
            s[:, j * 256 : (j + 1) * 256] = part

    def finish(i, s, p):
        top = jnp.max(s[...], axis=1, keepdims=True)
        total = jnp.zeros((group, 1), jnp.float32)
        for j in range(window // 256):
            e = jnp.exp2((s[:, j * 256 : (j + 1) * 256] - top) * (score_scale * log2e))
            total = total + jnp.sum(e, axis=1, keepdims=True)
            p[:, j * 256 : (j + 1) * 256] = e.astype(jnp.bfloat16)
        acc = jnp.dot(p[...], keys[:, :latent], preferred_element_type=jnp.float32)
        lat[pl.ds(pl.multiple_of(i * group, group), group), :] = (acc / total).astype(jnp.bfloat16)

    q_copy(0).wait()
    scores(0, s_a)

    @pl.loop(0, groups // 2 - 1)
    def _(n):
        i = 2 * n
        q_copy(i + 1).wait()
        q_copy(i + 2).wait()
        scores(i + 1, s_b)
        finish(i, s_a, p_a)
        scores(i + 2, s_a)
        finish(i + 1, s_b, p_b)

    q_copy(groups - 1).wait()
    scores(groups - 1, s_b)
    finish(groups - 2, s_a, p_a)
    finish(groups - 1, s_b, p_b)

    wuv_copy.wait()
    for h in range(heads):
        ho[:, h * vdim : (h + 1) * vdim] = jnp.dot(
            lat[h * tok : (h + 1) * tok, :], wuv[h], preferred_element_type=jnp.float32
        ).astype(jnp.bfloat16)
    for k in range(peers):
        wo_copy(k).wait()
        outs[k][...] = jnp.dot(ho[...], wo[k], preferred_element_type=jnp.float32).astype(jnp.bfloat16)


def attention(info, q, own, received, mates, w_uv, w_o):
    hbm = pl.BlockSpec(memory_space=pl.ANY)
    vmem = pl.BlockSpec(memory_space=pltpu.VMEM)
    return pl.pallas_call(
        attend,
        out_shape=[jax.ShapeDtypeStruct((tok, columns), jnp.bfloat16)] * peers,
        in_specs=[pl.BlockSpec(memory_space=pltpu.SMEM)] + [hbm] * 13,
        out_specs=[vmem] * peers,
        scratch_shapes=[
            pltpu.VMEM((window, wide), jnp.bfloat16),
            pltpu.VMEM((heads * tok, wide), jnp.bfloat16),
            pltpu.VMEM((heads, latent, vdim), jnp.bfloat16),
            pltpu.VMEM((peers, heads * vdim, columns), jnp.bfloat16),
            pltpu.VMEM((group, window), jnp.float32),
            pltpu.VMEM((group, window), jnp.float32),
            pltpu.VMEM((group, window), jnp.bfloat16),
            pltpu.VMEM((group, window), jnp.bfloat16),
            pltpu.VMEM((tok, 256), jnp.float32),
            pltpu.VMEM((heads * tok, latent), jnp.bfloat16),
            pltpu.VMEM((tok, heads * vdim), jnp.bfloat16),
            pltpu.SemaphoreType.DMA((9,)),
            pltpu.SemaphoreType.DMA((groups,)),
            pltpu.SemaphoreType.DMA,
            pltpu.SemaphoreType.DMA((peers,)),
        ],
        compiler_params=pltpu.CompilerParams(vmem_limit_bytes=56 * 1024 * 1024),
        cost_estimate=pl.CostEstimate(
            flops=24_000_000_000, bytes_accessed=26_000_000, transcendentals=5_500_000
        ),
        name="attend",
    )(info, q, own, *received, *mates, w_uv, w_o)


def gather(own):
    ctx = lax.axis_index("ctx")
    y = (ctx // 2) % 4
    swap = functools.partial(lax.ppermute, axis_name="ctx", perm=[(i, i ^ 1) for i in range(16)])
    crossed = lax.ppermute(
        own,
        ("ctx", "head"),
        [(c * 8 + h, (c + 8) * 8 + (h ^ 1)) for c in range(8) for h in range(8)],
    )
    lane = lax.broadcasted_iota(jnp.int32, (tok, wide), 1)
    missing = (lane == width + 4).astype(jnp.bfloat16)
    r4 = jnp.where(ctx >= 8, crossed, missing)
    received = []
    for k in (1, 2, 3):
        perm = [(i, (i // 8) * 8 + (i % 8 + 2 * k) % 8) for i in range(16)]
        received.append(lax.ppermute(jnp.where(y + k < 4, own, r4), "ctx", perm))
    received.append(r4)
    mates = [swap(block) for block in [own] + received]
    return received, mates


def local(queries, latent_kv, doc_ids, w_uv, w_o):
    same = doc_ids[:, None] == jnp.arange(4, dtype=doc_ids.dtype)[None, :]
    own = jnp.concatenate(
        [latent_kv, 1.0 - same.astype(jnp.bfloat16), jnp.zeros((tok, wide - width - 4), jnp.bfloat16)], axis=1
    )
    penalty = jnp.concatenate(
        [
            jnp.where(same, -big, 0.0).astype(jnp.bfloat16),
            jnp.full((tok, 1), -big, jnp.bfloat16),
            jnp.zeros((tok, wide - width - 5), jnp.bfloat16),
        ],
        axis=1,
    )
    q = jnp.concatenate(
        [queries, jnp.broadcast_to(penalty[:, None, :], (tok, heads, wide - width))], axis=2
    )
    q = q.transpose(1, 0, 2).reshape(heads * tok, wide)
    received, mates = gather(own)
    head = lax.axis_index("head")
    info = jnp.stack([lax.axis_index("ctx") % 2, head]).astype(jnp.int32)
    parts = attention(info, q, own, received, mates, w_uv, w_o)
    total = parts[0].astype(jnp.float32)
    for k in range(1, peers):
        total = total + lax.ppermute(
            parts[k], "head", [(i, i ^ k) for i in range(peers)]
        ).astype(jnp.float32)
    return total.astype(jnp.bfloat16)


def solution(mesh):
    return jax.shard_map(
        local,
        mesh=mesh,
        in_specs=(
            P("ctx", "head", None),
            P("ctx", None),
            P("ctx"),
            P("head", None, None),
            P("head", None),
        ),
        out_specs=P("ctx", "head"),
        check_vma=False,
    )
```

```python
import functools

import jax
import jax.numpy as jnp
from jax import lax
from jax.experimental import pallas as pl
from jax.experimental.pallas import tpu as pltpu
from jax.sharding import PartitionSpec as P

score_scale = 0.07216878
log2e = 1.4426950408889634
tok, heads, width, latent, vdim = 192, 16, 576, 512, 128
wide = 640
back = 8
window = 1792
own_at = back * tok
group = 2 * tok
groups = heads * tok // group
big = 2.0**100
peers = 8
columns = 512


def attend(
    info, q_hbm, own, r1, r2, r3, r4, m0, m1, m2, m3, m4, wuv_hbm, wo_hbm, out, *rest
):
    keys, q, wuv, wo, s_a, s_b, p_a, p_b, bias, lat, ho, key_sem, q_sem, w_sem, wo_sem = rest
    core = info[0]

    def key_copy(src, block):
        return pltpu.make_async_copy(src, keys.at[pl.ds(block * tok, tok)], key_sem.at[block])

    for block, src in ((0, r4), (2, r3), (4, r2), (6, r1), (8, own)):
        key_copy(src, block).start()

    @pl.when(core == 0)
    def _():
        for block, src in ((1, m4), (3, m3), (5, m2), (7, m1)):
            key_copy(src, block).start()

    @pl.when(core != 0)
    def _():
        for block, src in ((1, m3), (3, m2), (5, m1), (7, m0)):
            key_copy(src, block).start()

    def q_copy(i):
        return pltpu.make_async_copy(
            q_hbm.at[pl.ds(i * group, group)], q.at[pl.ds(i * group, group)], q_sem.at[i]
        )

    def wo_copy(k):
        return pltpu.make_async_copy(wo_hbm.at[:, pl.ds(k * columns, columns)], wo.at[k], wo_sem.at[k])

    for i in range(groups):
        q_copy(i).start()
    wuv_copy = pltpu.make_async_copy(wuv_hbm, wuv, w_sem)
    wuv_copy.start()
    for k in range(peers):
        wo_copy(k).start()

    keys[pl.ds(9 * tok, window - 9 * tok), :] = jnp.zeros((window - 9 * tok, wide), jnp.bfloat16)
    bias[...] = jnp.where(
        lax.broadcasted_iota(jnp.int32, (tok, 256), 1) <= lax.broadcasted_iota(jnp.int32, (tok, 256), 0),
        0.0,
        -big,
    )
    for block in range(9):
        key_copy(own, block).wait()

    def scores(i, s):
        rows = q[pl.ds(pl.multiple_of(i * group, group), group), :]
        for j in range(window // 256):
            part = lax.dot_general(
                rows,
                keys[j * 256 : (j + 1) * 256, :],
                (((1,), (1,)), ((), ())),
                preferred_element_type=jnp.float32,
            )
            if j == own_at // 256:
                part = part + jnp.concatenate([bias[...], bias[...]], axis=0)
            s[:, j * 256 : (j + 1) * 256] = part

    def finish(i, s, p):
        top = jnp.max(s[...], axis=1, keepdims=True)
        total = jnp.zeros((group, 1), jnp.float32)
        for j in range(window // 256):
            e = jnp.exp2((s[:, j * 256 : (j + 1) * 256] - top) * (score_scale * log2e))
            total = total + jnp.sum(e, axis=1, keepdims=True)
            p[:, j * 256 : (j + 1) * 256] = e.astype(jnp.bfloat16)
        acc = jnp.dot(p[...], keys[:, :latent], preferred_element_type=jnp.float32)
        lat[pl.ds(pl.multiple_of(i * group, group), group), :] = (acc / total).astype(jnp.bfloat16)

    q_copy(0).wait()
    scores(0, s_a)

    @pl.loop(0, groups // 2 - 1)
    def _(n):
        i = 2 * n
        q_copy(i + 1).wait()
        q_copy(i + 2).wait()
        scores(i + 1, s_b)
        finish(i, s_a, p_a)
        scores(i + 2, s_a)
        finish(i + 1, s_b, p_b)

    q_copy(groups - 1).wait()
    scores(groups - 1, s_b)
    finish(groups - 2, s_a, p_a)
    finish(groups - 1, s_b, p_b)

    wuv_copy.wait()
    for h in range(heads):
        ho[:, h * vdim : (h + 1) * vdim] = jnp.dot(
            lat[h * tok : (h + 1) * tok, :], wuv[h], preferred_element_type=jnp.float32
        ).astype(jnp.bfloat16)
    for k in range(peers):
        wo_copy(k).wait()
        out[k] = jnp.dot(ho[...], wo[k], preferred_element_type=jnp.float32).astype(jnp.bfloat16)


def attention(info, q, own, received, mates, w_uv, w_o):
    hbm = pl.BlockSpec(memory_space=pl.ANY)
    vmem = pl.BlockSpec(memory_space=pltpu.VMEM)
    return pl.pallas_call(
        attend,
        out_shape=jax.ShapeDtypeStruct((peers, tok, columns), jnp.bfloat16),
        in_specs=[pl.BlockSpec(memory_space=pltpu.SMEM)] + [hbm] * 13,
        out_specs=vmem,
        scratch_shapes=[
            pltpu.VMEM((window, wide), jnp.bfloat16),
            pltpu.VMEM((heads * tok, wide), jnp.bfloat16),
            pltpu.VMEM((heads, latent, vdim), jnp.bfloat16),
            pltpu.VMEM((peers, heads * vdim, columns), jnp.bfloat16),
            pltpu.VMEM((group, window), jnp.float32),
            pltpu.VMEM((group, window), jnp.float32),
            pltpu.VMEM((group, window), jnp.bfloat16),
            pltpu.VMEM((group, window), jnp.bfloat16),
            pltpu.VMEM((tok, 256), jnp.float32),
            pltpu.VMEM((heads * tok, latent), jnp.bfloat16),
            pltpu.VMEM((tok, heads * vdim), jnp.bfloat16),
            pltpu.SemaphoreType.DMA((9,)),
            pltpu.SemaphoreType.DMA((groups,)),
            pltpu.SemaphoreType.DMA,
            pltpu.SemaphoreType.DMA((peers,)),
        ],
        compiler_params=pltpu.CompilerParams(vmem_limit_bytes=56 * 1024 * 1024),
        cost_estimate=pl.CostEstimate(
            flops=24_000_000_000, bytes_accessed=26_000_000, transcendentals=5_500_000
        ),
        name="attend",
    )(info, q, own, *received, *mates, w_uv, w_o)


def gather(own, q):
    ctx = lax.axis_index("ctx")
    y = (ctx // 2) % 4
    swap = functools.partial(lax.ppermute, axis_name="ctx", perm=[(i, i ^ 1) for i in range(16)])
    crossed = lax.ppermute(
        own,
        ("ctx", "head"),
        [(c * 8 + h, (c + 8) * 8 + (h ^ 1)) for c in range(8) for h in range(8)],
    )
    lane = lax.broadcasted_iota(jnp.int32, (tok, wide), 1)
    missing = (lane == width + 4).astype(jnp.bfloat16)
    r4 = jnp.where(ctx >= 8, crossed, missing)
    received = []
    for k in (1, 2, 3):
        perm = [(i, (i // 8) * 8 + (i % 8 + 2 * k) % 8) for i in range(16)]
        received.append(lax.ppermute(jnp.where(y + k < 4, own, r4), "ctx", perm))
    received[0], q = lax.optimization_barrier((received[0], q))
    received.append(r4)
    mates = [swap(block) for block in [own] + received]
    return received, mates, q


def local(queries, latent_kv, doc_ids, w_uv, w_o):
    same = doc_ids[:, None] == jnp.arange(4, dtype=doc_ids.dtype)[None, :]
    own = jnp.concatenate(
        [latent_kv, 1.0 - same.astype(jnp.bfloat16), jnp.zeros((tok, wide - width - 4), jnp.bfloat16)], axis=1
    )
    penalty = jnp.concatenate(
        [
            jnp.where(same, -big, 0.0).astype(jnp.bfloat16),
            jnp.full((tok, 1), -big, jnp.bfloat16),
            jnp.zeros((tok, wide - width - 5), jnp.bfloat16),
        ],
        axis=1,
    )
    q = jnp.concatenate(
        [queries, jnp.broadcast_to(penalty[:, None, :], (tok, heads, wide - width))], axis=2
    )
    q = q.transpose(1, 0, 2).reshape(heads * tok, wide)
    received, mates, q = gather(own, q)
    info = (lax.axis_index("ctx") % 2).astype(jnp.int32).reshape(1)
    parts = attention(info, q, own, received, mates, w_uv, w_o)
    parts = lax.all_to_all(parts, "head", 0, 0)
    return jnp.sum(parts.astype(jnp.float32), axis=0).astype(jnp.bfloat16)


def solution(mesh):
    return jax.shard_map(
        local,
        mesh=mesh,
        in_specs=(
            P("ctx", "head", None),
            P("ctx", None),
            P("ctx"),
            P("head", None, None),
            P("head", None),
        ),
        out_specs=P("ctx", "head"),
        check_vma=False,
    )
```

```python
import functools

import jax
import jax.numpy as jnp
from jax import lax
from jax.experimental import pallas as pl
from jax.experimental.pallas import tpu as pltpu
from jax.sharding import PartitionSpec as P

score_scale = 0.07216878
log2e = 1.4426950408889634
tok, heads, width, latent, vdim = 192, 16, 576, 512, 128
wide = 640
back = 8
window = 1792
own_at = back * tok
group = 2 * tok
groups = heads * tok // group
big = 2.0**100
peers = 8
columns = 512


def attend(
    info, q, own, r1, r2, r3, r4, m0, m1, m2, m3, m4, wuv, wo, out, *rest
):
    keys, s_a, s_b, p_a, p_b, bias, lat, ho, key_sem = rest
    core, ctx = info[0], info[1]

    def key_copy(src, block):
        return pltpu.make_async_copy(src, keys.at[pl.ds(block * tok, tok)], key_sem.at[block])

    for block, src in ((0, r4), (2, r3), (4, r2), (6, r1), (8, own)):
        key_copy(src, block).start()

    @pl.when(core == 0)
    def _():
        for block, src in ((1, m4), (3, m3), (5, m2), (7, m1)):
            key_copy(src, block).start()

    @pl.when(core != 0)
    def _():
        for block, src in ((1, m3), (3, m2), (5, m1), (7, m0)):
            key_copy(src, block).start()

    keys[pl.ds(9 * tok, window - 9 * tok), :] = jnp.zeros((window - 9 * tok, wide), jnp.bfloat16)
    bias[...] = jnp.where(
        lax.broadcasted_iota(jnp.int32, (tok, 256), 1) <= lax.broadcasted_iota(jnp.int32, (tok, 256), 0),
        0.0,
        -big,
    )
    for block in range(9):
        key_copy(own, block).wait()
    missing = (lax.broadcasted_iota(jnp.int32, (tok, 128), 1) == width + 4 - latent).astype(jnp.bfloat16)
    for block in range(back):
        at = slice(block * tok, (block + 1) * tok)
        keys[at, latent:] = jnp.where(ctx + block < back, missing, keys[at, latent:])

    def scores(i, s):
        rows = q[pl.ds(pl.multiple_of(i * group, group), group), :]
        for j in range(window // 256):
            part = lax.dot_general(
                rows,
                keys[j * 256 : (j + 1) * 256, :],
                (((1,), (1,)), ((), ())),
                preferred_element_type=jnp.float32,
            )
            if j == own_at // 256:
                part = part + jnp.concatenate([bias[...], bias[...]], axis=0)
            s[:, j * 256 : (j + 1) * 256] = part

    def finish(i, s, p):
        top = jnp.max(s[...], axis=1, keepdims=True)
        total = jnp.zeros((group, 1), jnp.float32)
        for j in range(window // 256):
            e = jnp.exp2((s[:, j * 256 : (j + 1) * 256] - top) * (score_scale * log2e))
            total = total + jnp.sum(e, axis=1, keepdims=True)
            p[:, j * 256 : (j + 1) * 256] = e.astype(jnp.bfloat16)
        acc = jnp.dot(p[...], keys[:, :latent], preferred_element_type=jnp.float32)
        lat[pl.ds(pl.multiple_of(i * group, group), group), :] = (acc / total).astype(jnp.bfloat16)

    scores(0, s_a)

    @pl.loop(0, groups // 2 - 1)
    def _(n):
        i = 2 * n
        scores(i + 1, s_b)
        finish(i, s_a, p_a)
        scores(i + 2, s_a)
        finish(i + 1, s_b, p_b)

    scores(groups - 1, s_b)
    finish(groups - 2, s_a, p_a)
    finish(groups - 1, s_b, p_b)

    for h in range(heads):
        ho[:, h * vdim : (h + 1) * vdim] = jnp.dot(
            lat[h * tok : (h + 1) * tok, :], wuv[h], preferred_element_type=jnp.float32
        ).astype(jnp.bfloat16)
    for k in range(peers):
        out[k] = jnp.dot(ho[...], wo[:, k * columns : (k + 1) * columns], preferred_element_type=jnp.float32).astype(jnp.bfloat16)


def attention(info, q, own, received, mates, w_uv, w_o):
    vmem = pl.BlockSpec(memory_space=pltpu.VMEM)
    return pl.pallas_call(
        attend,
        out_shape=jax.ShapeDtypeStruct((peers, tok, columns), jnp.bfloat16),
        in_specs=[pl.BlockSpec(memory_space=pltpu.SMEM)] + [vmem] * 13,
        out_specs=vmem,
        scratch_shapes=[
            pltpu.VMEM((window, wide), jnp.bfloat16),
            pltpu.VMEM((group, window), jnp.float32),
            pltpu.VMEM((group, window), jnp.float32),
            pltpu.VMEM((group, window), jnp.bfloat16),
            pltpu.VMEM((group, window), jnp.bfloat16),
            pltpu.VMEM((tok, 256), jnp.float32),
            pltpu.VMEM((heads * tok, latent), jnp.bfloat16),
            pltpu.VMEM((tok, heads * vdim), jnp.bfloat16),
            pltpu.SemaphoreType.DMA((9,)),
        ],
        compiler_params=pltpu.CompilerParams(vmem_limit_bytes=24 * 1024 * 1024),
        cost_estimate=pl.CostEstimate(
            flops=24_000_000_000, bytes_accessed=26_000_000, transcendentals=5_500_000
        ),
        name="attend",
    )(info, q, own, *received, *mates, w_uv, w_o)


def gather(own, q):
    ctx = lax.axis_index("ctx")
    y = (ctx // 2) % 4
    swap = functools.partial(lax.ppermute, axis_name="ctx", perm=[(i, i ^ 1) for i in range(16)])
    crossed = lax.ppermute(
        own,
        ("ctx", "head"),
        [(c * 8 + h, (c + 8) * 8 + (h ^ 1)) for c in range(8) for h in range(8)],
    )
    received = []
    for k in (1, 2, 3):
        perm = [(i, (i // 8) * 8 + (i % 8 + 2 * k) % 8) for i in range(16)]
        received.append(lax.ppermute(jnp.where(y + k < 4, own, crossed), "ctx", perm))
    received[0], q = lax.optimization_barrier((received[0], q))
    received.append(crossed)
    mates = [swap(block) for block in [own] + received]
    return received, mates, q


def local(queries, latent_kv, doc_ids, w_uv, w_o):
    lane = lax.broadcasted_iota(jnp.int32, (tok, wide), 1) - width
    other = (lane >= 0) & (lane < 4) & (lane != doc_ids[:, None])
    own = jnp.where(other, 1.0, jnp.pad(latent_kv, ((0, 0), (0, wide - width)))).astype(jnp.bfloat16)
    lane = lax.broadcasted_iota(jnp.int32, (tok, wide - width), 1)
    penalty = jnp.where((lane == doc_ids[:, None]) | (lane == 4), -big, 0.0).astype(jnp.bfloat16)
    q = jnp.concatenate(
        [queries, jnp.broadcast_to(penalty[:, None, :], (tok, heads, wide - width))], axis=2
    )
    q = q.transpose(1, 0, 2).reshape(heads * tok, wide)
    received, mates, q = gather(own, q)
    ctx = lax.axis_index("ctx")
    info = jnp.stack([ctx % 2, ctx]).astype(jnp.int32)
    parts = attention(info, q, own, received, mates, w_uv, w_o)
    parts = lax.all_to_all(parts, "head", 0, 0)
    return jnp.sum(parts.astype(jnp.float32), axis=0).astype(jnp.bfloat16)


def solution(mesh):
    return jax.shard_map(
        local,
        mesh=mesh,
        in_specs=(
            P("ctx", "head", None),
            P("ctx", None),
            P("ctx"),
            P("head", None, None),
            P("head", None),
        ),
        out_specs=P("ctx", "head"),
        check_vma=False,
    )
```

```python
import functools

import jax
import jax.numpy as jnp
from jax import lax
from jax.experimental import pallas as pl
from jax.experimental.pallas import tpu as pltpu
from jax.sharding import PartitionSpec as P

score_scale = 0.07216878
log2e = 1.4426950408889634
tok, heads, width, latent, vdim = 192, 16, 576, 512, 128
wide = 640
back = 8
window = 1792
own_at = back * tok
group = 2 * tok
groups = heads * tok // group
big = 2.0**100
peers = 8
columns = 512


def attend(
    info, q, own, r1, r2, r3, r4, m0, m1, m2, m3, m4, wuv_hbm, wo_hbm, out, *rest
):
    keys, wuv, wo, s_a, s_b, p_a, p_b, bias, lat, ho, key_sem, w_sem, wo_sem = rest
    core, ctx = info[0], info[1]

    def key_copy(src, block):
        return pltpu.make_async_copy(src, keys.at[pl.ds(block * tok, tok)], key_sem.at[block])

    for block, src in ((0, r4), (2, r3), (4, r2), (6, r1), (8, own)):
        key_copy(src, block).start()

    @pl.when(core == 0)
    def _():
        for block, src in ((1, m4), (3, m3), (5, m2), (7, m1)):
            key_copy(src, block).start()

    @pl.when(core != 0)
    def _():
        for block, src in ((1, m3), (3, m2), (5, m1), (7, m0)):
            key_copy(src, block).start()

    wuv_copy = pltpu.make_async_copy(wuv_hbm, wuv, w_sem)

    def wo_copy(k):
        return pltpu.make_async_copy(wo_hbm.at[:, pl.ds(k * columns, columns)], wo.at[k], wo_sem.at[k])

    keys[pl.ds(9 * tok, window - 9 * tok), :] = jnp.zeros((window - 9 * tok, wide), jnp.bfloat16)
    bias[...] = jnp.where(
        lax.broadcasted_iota(jnp.int32, (tok, 256), 1) <= lax.broadcasted_iota(jnp.int32, (tok, 256), 0),
        0.0,
        -big,
    )
    for block in range(9):
        key_copy(own, block).wait()
    wuv_copy.start()
    for k in range(peers):
        wo_copy(k).start()
    missing = (lax.broadcasted_iota(jnp.int32, (tok, 128), 1) == width + 4 - latent).astype(jnp.bfloat16)
    for block in range(back):
        at = slice(block * tok, (block + 1) * tok)
        keys[at, latent:] = jnp.where(ctx + block < back, missing, keys[at, latent:])

    def scores(i, s):
        rows = q[pl.ds(pl.multiple_of(i * group, group), group), :]
        for j in range(window // 256):
            part = lax.dot_general(
                rows,
                keys[j * 256 : (j + 1) * 256, :],
                (((1,), (1,)), ((), ())),
                preferred_element_type=jnp.float32,
            )
            if j == own_at // 256:
                part = part + jnp.concatenate([bias[...], bias[...]], axis=0)
            s[:, j * 256 : (j + 1) * 256] = part

    def finish(i, s, p):
        top = jnp.max(s[...], axis=1, keepdims=True)
        total = jnp.zeros((group, 1), jnp.float32)
        for j in range(window // 256):
            e = jnp.exp2((s[:, j * 256 : (j + 1) * 256] - top) * (score_scale * log2e))
            total = total + jnp.sum(e, axis=1, keepdims=True)
            p[:, j * 256 : (j + 1) * 256] = e.astype(jnp.bfloat16)
        acc = jnp.dot(p[...], keys[:, :latent], preferred_element_type=jnp.float32)
        lat[pl.ds(pl.multiple_of(i * group, group), group), :] = (acc / total).astype(jnp.bfloat16)

    scores(0, s_a)

    @pl.loop(0, groups // 2 - 1)
    def _(n):
        i = 2 * n
        scores(i + 1, s_b)
        finish(i, s_a, p_a)
        scores(i + 2, s_a)
        finish(i + 1, s_b, p_b)

    scores(groups - 1, s_b)
    finish(groups - 2, s_a, p_a)
    finish(groups - 1, s_b, p_b)

    wuv_copy.wait()
    for h in range(heads):
        ho[:, h * vdim : (h + 1) * vdim] = jnp.dot(
            lat[h * tok : (h + 1) * tok, :], wuv[h], preferred_element_type=jnp.float32
        ).astype(jnp.bfloat16)
    for k in range(peers):
        wo_copy(k).wait()
        out[k] = jnp.dot(ho[...], wo[k], preferred_element_type=jnp.float32).astype(jnp.bfloat16)


def attention(info, q, own, received, mates, w_uv, w_o):
    hbm = pl.BlockSpec(memory_space=pl.ANY)
    vmem = pl.BlockSpec(memory_space=pltpu.VMEM)
    return pl.pallas_call(
        attend,
        out_shape=jax.ShapeDtypeStruct((peers, tok, columns), jnp.bfloat16),
        in_specs=[pl.BlockSpec(memory_space=pltpu.SMEM)] + [vmem] * 11 + [hbm] * 2,
        out_specs=vmem,
        scratch_shapes=[
            pltpu.VMEM((window, wide), jnp.bfloat16),
            pltpu.VMEM((heads, latent, vdim), jnp.bfloat16),
            pltpu.VMEM((peers, heads * vdim, columns), jnp.bfloat16),
            pltpu.VMEM((group, window), jnp.float32),
            pltpu.VMEM((group, window), jnp.float32),
            pltpu.VMEM((group, window), jnp.bfloat16),
            pltpu.VMEM((group, window), jnp.bfloat16),
            pltpu.VMEM((tok, 256), jnp.float32),
            pltpu.VMEM((heads * tok, latent), jnp.bfloat16),
            pltpu.VMEM((tok, heads * vdim), jnp.bfloat16),
            pltpu.SemaphoreType.DMA((9,)),
            pltpu.SemaphoreType.DMA,
            pltpu.SemaphoreType.DMA((peers,)),
        ],
        compiler_params=pltpu.CompilerParams(vmem_limit_bytes=42 * 1024 * 1024),
        cost_estimate=pl.CostEstimate(
            flops=24_000_000_000, bytes_accessed=26_000_000, transcendentals=5_500_000
        ),
        name="attend",
    )(info, q, own, *received, *mates, w_uv, w_o)


def gather(own, q):
    ctx = lax.axis_index("ctx")
    y = (ctx // 2) % 4
    swap = functools.partial(lax.ppermute, axis_name="ctx", perm=[(i, i ^ 1) for i in range(16)])
    crossed = lax.ppermute(
        own,
        ("ctx", "head"),
        [(c * 8 + h, (c + 8) * 8 + (h ^ 1)) for c in range(8) for h in range(8)],
    )
    received = []
    for k in (1, 2, 3):
        perm = [(i, (i // 8) * 8 + (i % 8 + 2 * k) % 8) for i in range(16)]
        received.append(lax.ppermute(jnp.where(y + k < 4, own, crossed), "ctx", perm))
    received[0], q = lax.optimization_barrier((received[0], q))
    received.append(crossed)
    mates = [swap(block) for block in [own] + received]
    return received, mates, q


def local(queries, latent_kv, doc_ids, w_uv, w_o):
    lane = lax.broadcasted_iota(jnp.int32, (tok, wide), 1) - width
    other = (lane >= 0) & (lane < 4) & (lane != doc_ids[:, None])
    own = jnp.where(other, 1.0, jnp.pad(latent_kv, ((0, 0), (0, wide - width)))).astype(jnp.bfloat16)
    lane = lax.broadcasted_iota(jnp.int32, (tok, wide - width), 1)
    penalty = jnp.where((lane == doc_ids[:, None]) | (lane == 4), -big, 0.0).astype(jnp.bfloat16)
    q = jnp.concatenate(
        [queries, jnp.broadcast_to(penalty[:, None, :], (tok, heads, wide - width))], axis=2
    )
    q = q.transpose(1, 0, 2).reshape(heads * tok, wide)
    received, mates, q = gather(own, q)
    ctx = lax.axis_index("ctx")
    info = jnp.stack([ctx % 2, ctx]).astype(jnp.int32)
    parts = attention(info, q, own, received, mates, w_uv, w_o)
    parts = lax.all_to_all(parts, "head", 0, 0)
    return jnp.sum(parts.astype(jnp.float32), axis=0).astype(jnp.bfloat16)


def solution(mesh):
    return jax.shard_map(
        local,
        mesh=mesh,
        in_specs=(
            P("ctx", "head", None),
            P("ctx", None),
            P("ctx"),
            P("head", None, None),
            P("head", None),
        ),
        out_specs=P("ctx", "head"),
        check_vma=False,
    )
```

```python
import functools

import jax
import jax.numpy as jnp
from jax import lax
from jax.experimental import pallas as pl
from jax.experimental.pallas import tpu as pltpu
from jax.sharding import PartitionSpec as P

score_scale = 0.07216878
log2e = 1.4426950408889634
tok, heads, width, latent, vdim = 192, 16, 576, 512, 128
wide = 640
back = 8
window = 1792
own_at = back * tok
group = 2 * tok
groups = heads * tok // group
big = 2.0**100
peers = 8
columns = 512


def attend(
    info, q_hbm, own, r1, r2, r3, r4, m0, m1, m2, m3, m4, wuv_hbm, wo_hbm, out, *rest
):
    keys, q, wuv, wo, s_a, s_b, p_a, p_b, bias, lat, ho, key_sem, q_sem, w_sem, wo_sem = rest
    core, ctx = info[0], info[1]

    def key_copy(src, block):
        return pltpu.make_async_copy(src, keys.at[pl.ds(block * tok, tok)], key_sem.at[block])

    for block, src in ((0, r4), (2, r3), (4, r2), (6, r1), (8, own)):
        key_copy(src, block).start()

    @pl.when(core == 0)
    def _():
        for block, src in ((1, m4), (3, m3), (5, m2), (7, m1)):
            key_copy(src, block).start()

    @pl.when(core != 0)
    def _():
        for block, src in ((1, m3), (3, m2), (5, m1), (7, m0)):
            key_copy(src, block).start()

    def q_copy(i):
        return pltpu.make_async_copy(
            q_hbm.at[pl.ds(i * group, group)], q.at[pl.ds(i * group, group)], q_sem.at[i]
        )

    def wo_copy(k):
        return pltpu.make_async_copy(wo_hbm.at[:, pl.ds(pl.multiple_of(k * columns, columns), columns)], wo.at[k], wo_sem.at[k])

    q_copy(0).start()
    wuv_copy = pltpu.make_async_copy(wuv_hbm, wuv, w_sem)

    keys[pl.ds(9 * tok, window - 9 * tok), :] = jnp.zeros((window - 9 * tok, wide), jnp.bfloat16)
    bias[...] = jnp.where(
        lax.broadcasted_iota(jnp.int32, (tok, 256), 1) <= lax.broadcasted_iota(jnp.int32, (tok, 256), 0),
        0.0,
        -big,
    )
    for block in range(9):
        key_copy(own, block).wait()
    q_copy(0).wait()
    for i in range(1, groups):
        q_copy(i).start()
    wuv_copy.start()
    for k in range(peers):
        wo_copy(k).start()
    missing = (lax.broadcasted_iota(jnp.int32, (tok, 128), 1) == width + 4 - latent).astype(jnp.bfloat16)
    for block in range(back):
        at = slice(block * tok, (block + 1) * tok)
        keys[at, latent:] = jnp.where(ctx + block < back, missing, keys[at, latent:])

    def scores(i, s):
        rows = q[pl.ds(pl.multiple_of(i * group, group), group), :]
        for j in range(window // 256):
            part = lax.dot_general(
                rows,
                keys[j * 256 : (j + 1) * 256, :],
                (((1,), (1,)), ((), ())),
                preferred_element_type=jnp.float32,
            )
            if j == own_at // 256:
                part = part + jnp.concatenate([bias[...], bias[...]], axis=0)
            s[:, j * 256 : (j + 1) * 256] = part

    def finish(i, s, p):
        top = jnp.max(s[...], axis=1, keepdims=True)
        total = jnp.zeros((group, 1), jnp.float32)
        for j in range(window // 256):
            e = jnp.exp2((s[:, j * 256 : (j + 1) * 256] - top) * (score_scale * log2e))
            total = total + jnp.sum(e, axis=1, keepdims=True)
            p[:, j * 256 : (j + 1) * 256] = e.astype(jnp.bfloat16)
        acc = jnp.dot(p[...], keys[:, :latent], preferred_element_type=jnp.float32)
        lat[pl.ds(pl.multiple_of(i * group, group), group), :] = (acc / total).astype(jnp.bfloat16)

    scores(0, s_a)

    @pl.loop(0, groups // 2 - 1)
    def _(n):
        i = 2 * n
        q_copy(i + 1).wait()
        q_copy(i + 2).wait()
        scores(i + 1, s_b)
        finish(i, s_a, p_a)
        scores(i + 2, s_a)
        finish(i + 1, s_b, p_b)

    q_copy(groups - 1).wait()
    scores(groups - 1, s_b)
    finish(groups - 2, s_a, p_a)
    finish(groups - 1, s_b, p_b)

    wuv_copy.wait()

    @pl.loop(0, heads // 4)
    def _(n):
        for u in range(4):
            h = 4 * n + u
            ho[:, pl.ds(pl.multiple_of(h * vdim, vdim), vdim)] = jnp.dot(
                lat[pl.ds(pl.multiple_of(h * tok, tok), tok), :], wuv[h], preferred_element_type=jnp.float32
            ).astype(jnp.bfloat16)

    @pl.loop(0, peers // 2)
    def _(n):
        wo_copy(2 * n).wait()
        wo_copy(2 * n + 1).wait()
        for u in range(2):
            k = 2 * n + u
            out[k] = jnp.dot(ho[...], wo[k], preferred_element_type=jnp.float32).astype(jnp.bfloat16)


def attention(info, q, own, received, mates, w_uv, w_o):
    hbm = pl.BlockSpec(memory_space=pl.ANY)
    vmem = pl.BlockSpec(memory_space=pltpu.VMEM)
    return pl.pallas_call(
        attend,
        out_shape=jax.ShapeDtypeStruct((peers, tok, columns), jnp.bfloat16),
        in_specs=[pl.BlockSpec(memory_space=pltpu.SMEM)] + [hbm] * 13,
        out_specs=vmem,
        scratch_shapes=[
            pltpu.VMEM((window, wide), jnp.bfloat16),
            pltpu.VMEM((heads * tok, wide), jnp.bfloat16),
            pltpu.VMEM((heads, latent, vdim), jnp.bfloat16),
            pltpu.VMEM((peers, heads * vdim, columns), jnp.bfloat16),
            pltpu.VMEM((group, window), jnp.float32),
            pltpu.VMEM((group, window), jnp.float32),
            pltpu.VMEM((group, window), jnp.bfloat16),
            pltpu.VMEM((group, window), jnp.bfloat16),
            pltpu.VMEM((tok, 256), jnp.float32),
            pltpu.VMEM((heads * tok, latent), jnp.bfloat16),
            pltpu.VMEM((tok, heads * vdim), jnp.bfloat16),
            pltpu.SemaphoreType.DMA((9,)),
            pltpu.SemaphoreType.DMA((groups,)),
            pltpu.SemaphoreType.DMA,
            pltpu.SemaphoreType.DMA((peers,)),
        ],
        compiler_params=pltpu.CompilerParams(vmem_limit_bytes=56 * 1024 * 1024),
        cost_estimate=pl.CostEstimate(
            flops=24_000_000_000, bytes_accessed=26_000_000, transcendentals=5_500_000
        ),
        name="attend",
    )(info, q, own, *received, *mates, w_uv, w_o)


def gather(own, q):
    ctx = lax.axis_index("ctx")
    y = (ctx // 2) % 4
    swap = functools.partial(lax.ppermute, axis_name="ctx", perm=[(i, i ^ 1) for i in range(16)])
    crossed = lax.ppermute(
        own,
        ("ctx", "head"),
        [(c * 8 + h, (c + 8) * 8 + (h ^ 1)) for c in range(8) for h in range(8)],
    )
    received = []
    for k in (1, 2, 3):
        perm = [(i, (i // 8) * 8 + (i % 8 + 2 * k) % 8) for i in range(16)]
        received.append(lax.ppermute(jnp.where(y + k < 4, own, crossed), "ctx", perm))
    received[0], q = lax.optimization_barrier((received[0], q))
    received.append(crossed)
    mates = [swap(block) for block in [own] + received]
    return received, mates, q


def local(queries, latent_kv, doc_ids, w_uv, w_o):
    lane = lax.broadcasted_iota(jnp.int32, (tok, wide), 1) - width
    other = (lane >= 0) & (lane < 4) & (lane != doc_ids[:, None])
    own = jnp.where(other, 1.0, jnp.pad(latent_kv, ((0, 0), (0, wide - width)))).astype(jnp.bfloat16)
    lane = lax.broadcasted_iota(jnp.int32, (tok, wide - width), 1)
    penalty = jnp.where((lane == doc_ids[:, None]) | (lane == 4), -big, 0.0).astype(jnp.bfloat16)
    q = jnp.concatenate(
        [queries, jnp.broadcast_to(penalty[:, None, :], (tok, heads, wide - width))], axis=2
    )
    q = q.transpose(1, 0, 2).reshape(heads * tok, wide)
    received, mates, q = gather(own, q)
    ctx = lax.axis_index("ctx")
    info = jnp.stack([ctx % 2, ctx]).astype(jnp.int32)
    parts = attention(info, q, own, received, mates, w_uv, w_o)
    parts = lax.all_to_all(parts, "head", 0, 0)
    return jnp.sum(parts.astype(jnp.float32), axis=0).astype(jnp.bfloat16)


def solution(mesh):
    return jax.shard_map(
        local,
        mesh=mesh,
        in_specs=(
            P("ctx", "head", None),
            P("ctx", None),
            P("ctx"),
            P("head", None, None),
            P("head", None),
        ),
        out_specs=P("ctx", "head"),
        check_vma=False,
    )
```

```python
import functools

import jax
import jax.numpy as jnp
from jax import lax
from jax.experimental import pallas as pl
from jax.experimental.pallas import tpu as pltpu
from jax.sharding import PartitionSpec as P

score_scale = 0.07216878
log2e = 1.4426950408889634
tok, heads, width, latent, vdim = 192, 16, 576, 512, 128
wide = 640
back = 8
window = 1792
own_at = back * tok
group = 2 * tok
groups = heads * tok // group
big = 2.0**100
peers = 8
columns = 512


def attend(
    info, q_hbm, own, r1, r2, r3, r4, m0, m1, m2, m3, m4, wuv_hbm, wo_hbm, out, *rest
):
    keys, q, wuv, wo, s_a, s_b, p_a, p_b, bias, lat, ho, made, key_sem, q_sem, w_sem, wo_sem, out_sem = rest
    core, ctx = info[0], info[1]

    def key_copy(src, block):
        return pltpu.make_async_copy(src, keys.at[pl.ds(block * tok, tok)], key_sem.at[block])

    for block, src in ((0, r4), (2, r3), (4, r2), (6, r1), (8, own)):
        key_copy(src, block).start()

    @pl.when(core == 0)
    def _():
        for block, src in ((1, m4), (3, m3), (5, m2), (7, m1)):
            key_copy(src, block).start()

    @pl.when(core != 0)
    def _():
        for block, src in ((1, m3), (3, m2), (5, m1), (7, m0)):
            key_copy(src, block).start()

    def q_copy(i):
        return pltpu.make_async_copy(
            q_hbm.at[pl.ds(i * group, group)], q.at[pl.ds(i * group, group)], q_sem.at[i]
        )

    def wo_copy(k):
        return pltpu.make_async_copy(wo_hbm.at[:, pl.ds(pl.multiple_of(k * columns, columns), columns)], wo.at[k], wo_sem.at[k])

    q_copy(0).start()
    wuv_copy = pltpu.make_async_copy(wuv_hbm, wuv, w_sem)

    keys[pl.ds(9 * tok, window - 9 * tok), :] = jnp.zeros((window - 9 * tok, wide), jnp.bfloat16)
    bias[...] = jnp.where(
        lax.broadcasted_iota(jnp.int32, (tok, 256), 1) <= lax.broadcasted_iota(jnp.int32, (tok, 256), 0),
        0.0,
        -big,
    )
    for block in range(9):
        key_copy(own, block).wait()
    q_copy(0).wait()
    for i in range(1, groups):
        q_copy(i).start()
    wuv_copy.start()
    for k in range(peers):
        wo_copy(k).start()
    missing = (lax.broadcasted_iota(jnp.int32, (tok, 128), 1) == width + 4 - latent).astype(jnp.bfloat16)
    for block in range(back):
        at = slice(block * tok, (block + 1) * tok)
        keys[at, latent:] = jnp.where(ctx + block < back, missing, keys[at, latent:])

    def scores(i, s):
        rows = q[pl.ds(pl.multiple_of(i * group, group), group), :]
        for j in range(window // 256):
            part = lax.dot_general(
                rows,
                keys[j * 256 : (j + 1) * 256, :],
                (((1,), (1,)), ((), ())),
                preferred_element_type=jnp.float32,
            )
            if j == own_at // 256:
                part = part + jnp.concatenate([bias[...], bias[...]], axis=0)
            s[:, j * 256 : (j + 1) * 256] = part

    def finish(i, s, p):
        top = jnp.max(s[...], axis=1, keepdims=True)
        total = jnp.zeros((group, 1), jnp.float32)
        for j in range(window // 256):
            e = jnp.exp2((s[:, j * 256 : (j + 1) * 256] - top) * (score_scale * log2e))
            total = total + jnp.sum(e, axis=1, keepdims=True)
            p[:, j * 256 : (j + 1) * 256] = e.astype(jnp.bfloat16)
        acc = jnp.dot(p[...], keys[:, :latent], preferred_element_type=jnp.float32)
        lat[pl.ds(pl.multiple_of(i * group, group), group), :] = (acc / total).astype(jnp.bfloat16)

    scores(0, s_a)

    @pl.loop(0, groups // 2 - 1)
    def _(n):
        i = 2 * n
        q_copy(i + 1).wait()
        q_copy(i + 2).wait()
        scores(i + 1, s_b)
        finish(i, s_a, p_a)
        scores(i + 2, s_a)
        finish(i + 1, s_b, p_b)

    q_copy(groups - 1).wait()
    scores(groups - 1, s_b)
    finish(groups - 2, s_a, p_a)
    finish(groups - 1, s_b, p_b)

    wuv_copy.wait()

    @pl.loop(0, heads // 4)
    def _(n):
        for u in range(4):
            h = 4 * n + u
            ho[:, pl.ds(pl.multiple_of(h * vdim, vdim), vdim)] = jnp.dot(
                lat[pl.ds(pl.multiple_of(h * tok, tok), tok), :], wuv[h], preferred_element_type=jnp.float32
            ).astype(jnp.bfloat16)

    def out_copy(k):
        return pltpu.make_async_copy(made.at[k], out.at[k], out_sem.at[k])

    @pl.loop(0, peers // 2)
    def _(n):
        wo_copy(2 * n).wait()
        wo_copy(2 * n + 1).wait()
        for u in range(2):
            k = 2 * n + u
            made[k] = jnp.dot(ho[...], wo[k], preferred_element_type=jnp.float32).astype(jnp.bfloat16)
            out_copy(k).start()

    for k in range(peers):
        out_copy(k).wait()


def attention(info, q, own, received, mates, w_uv, w_o):
    hbm = pl.BlockSpec(memory_space=pl.ANY)
    vmem = pl.BlockSpec(memory_space=pltpu.VMEM)
    return pl.pallas_call(
        attend,
        out_shape=jax.ShapeDtypeStruct((peers, tok, columns), jnp.bfloat16),
        in_specs=[pl.BlockSpec(memory_space=pltpu.SMEM)] + [hbm] * 13,
        out_specs=hbm,
        scratch_shapes=[
            pltpu.VMEM((window, wide), jnp.bfloat16),
            pltpu.VMEM((heads * tok, wide), jnp.bfloat16),
            pltpu.VMEM((heads, latent, vdim), jnp.bfloat16),
            pltpu.VMEM((peers, heads * vdim, columns), jnp.bfloat16),
            pltpu.VMEM((group, window), jnp.float32),
            pltpu.VMEM((group, window), jnp.float32),
            pltpu.VMEM((group, window), jnp.bfloat16),
            pltpu.VMEM((group, window), jnp.bfloat16),
            pltpu.VMEM((tok, 256), jnp.float32),
            pltpu.VMEM((heads * tok, latent), jnp.bfloat16),
            pltpu.VMEM((tok, heads * vdim), jnp.bfloat16),
            pltpu.VMEM((peers, tok, columns), jnp.bfloat16),
            pltpu.SemaphoreType.DMA((9,)),
            pltpu.SemaphoreType.DMA((groups,)),
            pltpu.SemaphoreType.DMA,
            pltpu.SemaphoreType.DMA((peers,)),
            pltpu.SemaphoreType.DMA((peers,)),
        ],
        compiler_params=pltpu.CompilerParams(vmem_limit_bytes=56 * 1024 * 1024),
        cost_estimate=pl.CostEstimate(
            flops=24_000_000_000, bytes_accessed=26_000_000, transcendentals=5_500_000
        ),
        name="attend",
    )(info, q, own, *received, *mates, w_uv, w_o)


def gather(own, q, info):
    ctx = lax.axis_index("ctx")
    y = (ctx // 2) % 4
    swap = functools.partial(lax.ppermute, axis_name="ctx", perm=[(i, i ^ 1) for i in range(16)])
    crossed = lax.ppermute(
        own,
        ("ctx", "head"),
        [(c * 8 + h, (c + 8) * 8 + (h ^ 1)) for c in range(8) for h in range(8)],
    )
    received = []
    for k in (1, 2, 3):
        perm = [(i, (i // 8) * 8 + (i % 8 + 2 * k) % 8) for i in range(16)]
        received.append(lax.ppermute(jnp.where(y + k < 4, own, crossed), "ctx", perm))
    received[0], q, info = lax.optimization_barrier((received[0], q, info))
    received.append(crossed)
    mates = [swap(block) for block in [own] + received]
    return received, mates, q, info


def local(queries, latent_kv, doc_ids, w_uv, w_o):
    lane = lax.broadcasted_iota(jnp.int32, (tok, wide), 1) - width
    other = (lane >= 0) & (lane < 4) & (lane != doc_ids[:, None])
    own = jnp.where(other, 1.0, jnp.pad(latent_kv, ((0, 0), (0, wide - width)))).astype(jnp.bfloat16)
    lane = lax.broadcasted_iota(jnp.int32, (tok, wide - width), 1)
    penalty = jnp.where((lane == doc_ids[:, None]) | (lane == 4), -big, 0.0).astype(jnp.bfloat16)
    q = jnp.concatenate(
        [queries, jnp.broadcast_to(penalty[:, None, :], (tok, heads, wide - width))], axis=2
    )
    q = q.transpose(1, 0, 2).reshape(heads * tok, wide)
    ctx = lax.axis_index("ctx")
    info = jnp.stack([ctx % 2, ctx]).astype(jnp.int32)
    received, mates, q, info = gather(own, q, info)
    parts = attention(info, q, own, received, mates, w_uv, w_o)
    parts = lax.all_to_all(parts, "head", 0, 0)
    return jnp.sum(parts.astype(jnp.float32), axis=0).astype(jnp.bfloat16)


def solution(mesh):
    return jax.shard_map(
        local,
        mesh=mesh,
        in_specs=(
            P("ctx", "head", None),
            P("ctx", None),
            P("ctx"),
            P("head", None, None),
            P("head", None),
        ),
        out_specs=P("ctx", "head"),
        check_vma=False,
    )
```

```python
import functools

import jax
import jax.numpy as jnp
from jax import lax
from jax.experimental import pallas as pl
from jax.experimental.pallas import tpu as pltpu
from jax.sharding import PartitionSpec as P

score_scale = 0.07216878
log2e = 1.4426950408889634
tok, heads, width, latent, vdim = 192, 16, 576, 512, 128
wide = 640
back = 8
window = 1792
own_at = back * tok
group = 2 * tok
groups = heads * tok // group
big = 2.0**100
peers = 8
columns = 512


def attend(
    info, q_hbm, own, r1, r2, r3, r4, m0, m1, m2, m3, m4, wuv_hbm, wo_hbm, out, *rest
):
    keys, q, wuv, wo, s_a, s_b, p_a, p_b, bias, lat, ho, made, key_sem, q_sem, w_sem, wo_sem, out_sem = rest
    core, ctx = info[0], info[1]

    def key_copy(src, block):
        return pltpu.make_async_copy(src, keys.at[pl.ds(block * tok, tok)], key_sem.at[block])

    for block, src in ((0, r4), (2, r3), (4, r2), (6, r1), (8, own)):
        key_copy(src, block).start()

    @pl.when(core == 0)
    def _():
        for block, src in ((1, m4), (3, m3), (5, m2), (7, m1)):
            key_copy(src, block).start()

    @pl.when(core != 0)
    def _():
        for block, src in ((1, m3), (3, m2), (5, m1), (7, m0)):
            key_copy(src, block).start()

    def q_copy(i):
        return pltpu.make_async_copy(
            q_hbm.at[pl.ds(i * group, group)], q.at[pl.ds(i * group, group)], q_sem.at[i]
        )

    def wo_copy(k):
        return pltpu.make_async_copy(wo_hbm.at[:, pl.ds(pl.multiple_of(k * columns, columns), columns)], wo.at[k], wo_sem.at[k])

    q_copy(0).start()
    wuv_copy = pltpu.make_async_copy(wuv_hbm, wuv, w_sem)

    keys[pl.ds(9 * tok, window - 9 * tok), :] = jnp.zeros((window - 9 * tok, wide), jnp.bfloat16)
    bias[...] = jnp.where(
        lax.broadcasted_iota(jnp.int32, (tok, 256), 1) <= lax.broadcasted_iota(jnp.int32, (tok, 256), 0),
        0.0,
        -big,
    )
    for block in range(9):
        key_copy(own, block).wait()
    q_copy(0).wait()
    for i in range(1, groups):
        q_copy(i).start()
    wuv_copy.start()
    for k in range(peers):
        wo_copy(k).start()
    missing = (lax.broadcasted_iota(jnp.int32, (tok, 128), 1) == width + 4 - latent).astype(jnp.bfloat16)
    for block in range(back):
        at = slice(block * tok, (block + 1) * tok)
        keys[at, latent:] = jnp.where(ctx + block < back, missing, keys[at, latent:])

    def scores(i, s):
        rows = q[pl.ds(pl.multiple_of(i * group, group), group), :]
        for j in range(window // 256):
            part = lax.dot_general(
                rows,
                keys[j * 256 : (j + 1) * 256, :],
                (((1,), (1,)), ((), ())),
                preferred_element_type=jnp.float32,
            )
            if j == own_at // 256:
                part = part + jnp.concatenate([bias[...], bias[...]], axis=0)
            s[:, j * 256 : (j + 1) * 256] = part

    def finish(i, s, p):
        top = jnp.max(s[...], axis=1, keepdims=True)
        total = jnp.zeros((group, 1), jnp.float32)
        for j in range(window // 256):
            e = jnp.exp2((s[:, j * 256 : (j + 1) * 256] - top) * (score_scale * log2e))
            total = total + jnp.sum(e, axis=1, keepdims=True)
            p[:, j * 256 : (j + 1) * 256] = e.astype(jnp.bfloat16)
        acc = jnp.dot(p[...], keys[:, :latent], preferred_element_type=jnp.float32)
        lat[pl.ds(pl.multiple_of(i * group, group), group), :] = (acc / total).astype(jnp.bfloat16)

    scores(0, s_a)

    @pl.loop(0, groups // 2 - 1)
    def _(n):
        i = 2 * n
        q_copy(i + 1).wait()
        q_copy(i + 2).wait()
        scores(i + 1, s_b)
        finish(i, s_a, p_a)
        scores(i + 2, s_a)
        finish(i + 1, s_b, p_b)

    q_copy(groups - 1).wait()
    scores(groups - 1, s_b)
    finish(groups - 2, s_a, p_a)
    finish(groups - 1, s_b, p_b)

    wuv_copy.wait()

    @pl.loop(0, heads // 4)
    def _(n):
        for u in range(4):
            h = 4 * n + u
            ho[:, pl.ds(pl.multiple_of(h * vdim, vdim), vdim)] = jnp.dot(
                lat[pl.ds(pl.multiple_of(h * tok, tok), tok), :], wuv[h], preferred_element_type=jnp.float32
            ).astype(jnp.bfloat16)

    def out_copy(k):
        return pltpu.make_async_copy(made.at[k], out.at[k], out_sem.at[k])

    @pl.loop(0, peers // 2)
    def _(n):
        wo_copy(2 * n).wait()
        wo_copy(2 * n + 1).wait()
        for u in range(2):
            k = 2 * n + u
            made[k] = jnp.dot(ho[...], wo[k], preferred_element_type=jnp.float32).astype(jnp.bfloat16)
            out_copy(k).start()

    for k in range(peers):
        out_copy(k).wait()


def attention(info, q, own, received, mates, w_uv, w_o):
    hbm = pl.BlockSpec(memory_space=pl.ANY)
    vmem = pl.BlockSpec(memory_space=pltpu.VMEM)
    return pl.pallas_call(
        attend,
        out_shape=jax.ShapeDtypeStruct((peers, tok, columns), jnp.bfloat16),
        in_specs=[pl.BlockSpec(memory_space=pltpu.SMEM)] + [hbm] * 13,
        out_specs=hbm,
        scratch_shapes=[
            pltpu.VMEM((window, wide), jnp.bfloat16),
            pltpu.VMEM((heads * tok, wide), jnp.bfloat16),
            pltpu.VMEM((heads, latent, vdim), jnp.bfloat16),
            pltpu.VMEM((peers, heads * vdim, columns), jnp.bfloat16),
            pltpu.VMEM((group, window), jnp.float32),
            pltpu.VMEM((group, window), jnp.float32),
            pltpu.VMEM((group, window), jnp.bfloat16),
            pltpu.VMEM((group, window), jnp.bfloat16),
            pltpu.VMEM((tok, 256), jnp.float32),
            pltpu.VMEM((heads * tok, latent), jnp.bfloat16),
            pltpu.VMEM((tok, heads * vdim), jnp.bfloat16),
            pltpu.VMEM((peers, tok, columns), jnp.bfloat16),
            pltpu.SemaphoreType.DMA((9,)),
            pltpu.SemaphoreType.DMA((groups,)),
            pltpu.SemaphoreType.DMA,
            pltpu.SemaphoreType.DMA((peers,)),
            pltpu.SemaphoreType.DMA((peers,)),
        ],
        compiler_params=pltpu.CompilerParams(vmem_limit_bytes=56 * 1024 * 1024),
        cost_estimate=pl.CostEstimate(
            flops=24_000_000_000, bytes_accessed=26_000_000, transcendentals=5_500_000
        ),
        name="attend",
    )(info, q, own, *received, *mates, w_uv, w_o)


def extend(block, docs):
    lane = lax.broadcasted_iota(jnp.int32, (tok, wide), 1) - width
    other = (lane >= 0) & (lane < 4) & (lane != docs.astype(jnp.int32)[:, None])
    return jnp.where(other, 1.0, jnp.pad(block, ((0, 0), (0, wide - width)))).astype(jnp.bfloat16)


def gather(latent_kv, doc_ids, q, info):
    ctx = lax.axis_index("ctx")
    y = (ctx // 2) % 4
    swap = functools.partial(lax.ppermute, axis_name="ctx", perm=[(i, i ^ 1) for i in range(16)])
    cross = functools.partial(
        lax.ppermute,
        axis_name=("ctx", "head"),
        perm=[(c * 8 + h, (c + 8) * 8 + (h ^ 1)) for c in range(8) for h in range(8)],
    )
    docs = doc_ids.astype(jnp.bfloat16)
    moved, moved_docs = cross(latent_kv), cross(docs)
    own, moved = lax.optimization_barrier((extend(latent_kv, docs), moved))
    crossed = extend(moved, moved_docs)
    later, later_docs = lax.optimization_barrier((moved, moved_docs))
    received = {}
    for k in (2, 1, 3):
        perm = [(i, (i // 8) * 8 + (i % 8 + 2 * k) % 8) for i in range(16)]
        received[k] = lax.ppermute(jnp.where(y + k < 4, own, crossed), "ctx", perm)
    received[1], q, info = lax.optimization_barrier((received[1], q, info))
    received = [received[1], received[2], received[3], extend(later, later_docs)]
    mates = [swap(block) for block in [own] + received]
    return own, received, mates, q, info


def local(queries, latent_kv, doc_ids, w_uv, w_o):
    lane = lax.broadcasted_iota(jnp.int32, (tok, wide - width), 1)
    penalty = jnp.where((lane == doc_ids[:, None]) | (lane == 4), -big, 0.0).astype(jnp.bfloat16)
    q = jnp.concatenate(
        [queries, jnp.broadcast_to(penalty[:, None, :], (tok, heads, wide - width))], axis=2
    )
    q = q.transpose(1, 0, 2).reshape(heads * tok, wide)
    ctx = lax.axis_index("ctx")
    info = jnp.stack([ctx % 2, ctx]).astype(jnp.int32)
    own, received, mates, q, info = gather(latent_kv, doc_ids, q, info)
    parts = attention(info, q, own, received, mates, w_uv, w_o)
    parts = lax.all_to_all(parts, "head", 0, 0)
    return jnp.sum(parts.astype(jnp.float32), axis=0).astype(jnp.bfloat16)


def solution(mesh):
    return jax.shard_map(
        local,
        mesh=mesh,
        in_specs=(
            P("ctx", "head", None),
            P("ctx", None),
            P("ctx"),
            P("head", None, None),
            P("head", None),
        ),
        out_specs=P("ctx", "head"),
        check_vma=False,
    )
```

```python
import functools

import jax
import jax.numpy as jnp
from jax import lax
from jax.experimental import pallas as pl
from jax.experimental.pallas import tpu as pltpu
from jax.sharding import PartitionSpec as P

score_scale = 0.07216878
log2e = 1.4426950408889634
tok, heads, width, latent, vdim = 192, 16, 576, 512, 128
wide = 640
back = 8
window = 1792
own_at = back * tok
group = 2 * tok
groups = heads * tok // group
big = 2.0**100
peers = 8
columns = 512


def attend(
    info, q_hbm, own, r1, r2, r3, r4, m0, m1, m2, m3, m4, wuv_hbm, wo_hbm, out, *rest
):
    keys, q, wuv, wo, s_a, s_b, p_a, p_b, bias, lat, ho, made, key_sem, q_sem, w_sem, wo_sem, out_sem = rest
    core, ctx = info[0], info[1]

    def key_copy(src, block, sem):
        return pltpu.make_async_copy(src, keys.at[pl.ds(block * tok, tok)], key_sem.at[sem])

    for block, src in ((0, r4), (6, r1), (8, own)):
        key_copy(src, block, block).start()

    @pl.when(core == 0)
    def _():
        for block, src, sem in ((1, m4, 1), (7, m1, 7)):
            key_copy(src, block, sem).start()

    @pl.when(core != 0)
    def _():
        for block, src, sem in ((5, m1, 1), (7, m0, 7)):
            key_copy(src, block, sem).start()

    def q_copy(i):
        return pltpu.make_async_copy(
            q_hbm.at[pl.ds(i * group, group)], q.at[pl.ds(i * group, group)], q_sem.at[i]
        )

    def wo_copy(k):
        return pltpu.make_async_copy(wo_hbm.at[:, pl.ds(pl.multiple_of(k * columns, columns), columns)], wo.at[k], wo_sem.at[k])

    q_copy(0).start()
    wuv_copy = pltpu.make_async_copy(wuv_hbm, wuv, w_sem)

    keys[pl.ds(9 * tok, window - 9 * tok), :] = jnp.zeros((window - 9 * tok, wide), jnp.bfloat16)
    bias[...] = jnp.where(
        lax.broadcasted_iota(jnp.int32, (tok, 256), 1) <= lax.broadcasted_iota(jnp.int32, (tok, 256), 0),
        0.0,
        -big,
    )
    for block in (0, 1, 6, 7, 8):
        key_copy(own, block, block).wait()
    first = pl.multiple_of(jnp.where(core == 0, 3 * tok, tok), tok)
    keys[2 * tok : 3 * tok, :] = r3[...]
    keys[4 * tok : 5 * tok, :] = r2[...]
    keys[pl.ds(first, tok), :] = m3[...]
    keys[pl.ds(pl.multiple_of(first + 2 * tok, tok), tok), :] = m2[...]
    q_copy(0).wait()
    for i in range(1, groups):
        q_copy(i).start()
    wuv_copy.start()
    for k in range(peers):
        wo_copy(k).start()
    missing = (lax.broadcasted_iota(jnp.int32, (tok, 128), 1) == width + 4 - latent).astype(jnp.bfloat16)
    for block in range(back):
        at = slice(block * tok, (block + 1) * tok)
        keys[at, latent:] = jnp.where(ctx + block < back, missing, keys[at, latent:])

    def scores(i, s):
        rows = q[pl.ds(pl.multiple_of(i * group, group), group), :]
        for j in range(window // 256):
            part = lax.dot_general(
                rows,
                keys[j * 256 : (j + 1) * 256, :],
                (((1,), (1,)), ((), ())),
                preferred_element_type=jnp.float32,
            )
            if j == own_at // 256:
                part = part + jnp.concatenate([bias[...], bias[...]], axis=0)
            s[:, j * 256 : (j + 1) * 256] = part

    def finish(i, s, p):
        top = jnp.max(s[...], axis=1, keepdims=True)
        total = jnp.zeros((group, 1), jnp.float32)
        for j in range(window // 256):
            e = jnp.exp2((s[:, j * 256 : (j + 1) * 256] - top) * (score_scale * log2e))
            total = total + jnp.sum(e, axis=1, keepdims=True)
            p[:, j * 256 : (j + 1) * 256] = e.astype(jnp.bfloat16)
        acc = jnp.dot(p[...], keys[:, :latent], preferred_element_type=jnp.float32)
        lat[pl.ds(pl.multiple_of(i * group, group), group), :] = (acc / total).astype(jnp.bfloat16)

    scores(0, s_a)

    @pl.loop(0, groups // 2 - 1)
    def _(n):
        i = 2 * n
        q_copy(i + 1).wait()
        q_copy(i + 2).wait()
        scores(i + 1, s_b)
        finish(i, s_a, p_a)
        scores(i + 2, s_a)
        finish(i + 1, s_b, p_b)

    q_copy(groups - 1).wait()
    scores(groups - 1, s_b)
    finish(groups - 2, s_a, p_a)
    finish(groups - 1, s_b, p_b)

    wuv_copy.wait()

    @pl.loop(0, heads // 4)
    def _(n):
        for u in range(4):
            h = 4 * n + u
            ho[:, pl.ds(pl.multiple_of(h * vdim, vdim), vdim)] = jnp.dot(
                lat[pl.ds(pl.multiple_of(h * tok, tok), tok), :], wuv[h], preferred_element_type=jnp.float32
            ).astype(jnp.bfloat16)

    def out_copy(k):
        return pltpu.make_async_copy(made.at[k], out.at[k], out_sem.at[k])

    @pl.loop(0, peers // 2)
    def _(n):
        wo_copy(2 * n).wait()
        wo_copy(2 * n + 1).wait()
        for u in range(2):
            k = 2 * n + u
            made[k] = jnp.dot(ho[...], wo[k], preferred_element_type=jnp.float32).astype(jnp.bfloat16)
            out_copy(k).start()

    for k in range(peers):
        out_copy(k).wait()


def attention(info, q, own, received, mates, w_uv, w_o):
    hbm = pl.BlockSpec(memory_space=pl.ANY)
    vmem = pl.BlockSpec(memory_space=pltpu.VMEM)
    return pl.pallas_call(
        attend,
        out_shape=jax.ShapeDtypeStruct((peers, tok, columns), jnp.bfloat16),
        in_specs=[pl.BlockSpec(memory_space=pltpu.SMEM)] + [hbm] * 3 + [vmem] * 2 + [hbm] * 3 + [vmem] * 2 + [hbm] * 3,
        out_specs=hbm,
        scratch_shapes=[
            pltpu.VMEM((window, wide), jnp.bfloat16),
            pltpu.VMEM((heads * tok, wide), jnp.bfloat16),
            pltpu.VMEM((heads, latent, vdim), jnp.bfloat16),
            pltpu.VMEM((peers, heads * vdim, columns), jnp.bfloat16),
            pltpu.VMEM((group, window), jnp.float32),
            pltpu.VMEM((group, window), jnp.float32),
            pltpu.VMEM((group, window), jnp.bfloat16),
            pltpu.VMEM((group, window), jnp.bfloat16),
            pltpu.VMEM((tok, 256), jnp.float32),
            pltpu.VMEM((heads * tok, latent), jnp.bfloat16),
            pltpu.VMEM((tok, heads * vdim), jnp.bfloat16),
            pltpu.VMEM((peers, tok, columns), jnp.bfloat16),
            pltpu.SemaphoreType.DMA((9,)),
            pltpu.SemaphoreType.DMA((groups,)),
            pltpu.SemaphoreType.DMA,
            pltpu.SemaphoreType.DMA((peers,)),
            pltpu.SemaphoreType.DMA((peers,)),
        ],
        compiler_params=pltpu.CompilerParams(vmem_limit_bytes=50 * 1024 * 1024),
        cost_estimate=pl.CostEstimate(
            flops=24_000_000_000, bytes_accessed=26_000_000, transcendentals=5_500_000
        ),
        name="attend",
    )(info, q, own, *received, *mates, w_uv, w_o)


def extend(block, docs):
    lane = lax.broadcasted_iota(jnp.int32, (tok, wide), 1) - width
    other = (lane >= 0) & (lane < 4) & (lane != docs.astype(jnp.int32)[:, None])
    return jnp.where(other, 1.0, jnp.pad(block, ((0, 0), (0, wide - width)))).astype(jnp.bfloat16)


def gather(latent_kv, doc_ids, q, info):
    ctx = lax.axis_index("ctx")
    y = (ctx // 2) % 4
    swap = functools.partial(lax.ppermute, axis_name="ctx", perm=[(i, i ^ 1) for i in range(16)])
    cross = functools.partial(
        lax.ppermute,
        axis_name=("ctx", "head"),
        perm=[(c * 8 + h, (c + 8) * 8 + (h ^ 1)) for c in range(8) for h in range(8)],
    )
    docs = doc_ids.astype(jnp.bfloat16)
    moved, moved_docs = cross(latent_kv), cross(docs)
    own, moved = lax.optimization_barrier((extend(latent_kv, docs), moved))
    crossed = extend(moved, moved_docs)
    later, later_docs = lax.optimization_barrier((moved, moved_docs))
    received = {}
    for k in (2, 1, 3):
        perm = [(i, (i // 8) * 8 + (i % 8 + 2 * k) % 8) for i in range(16)]
        received[k] = lax.ppermute(jnp.where(y + k < 4, own, crossed), "ctx", perm)
    received[1], q, info = lax.optimization_barrier((received[1], q, info))
    received = [received[1], received[2], received[3], extend(later, later_docs)]
    mates = [swap(block) for block in [own] + received]
    return own, received, mates, q, info


def local(queries, latent_kv, doc_ids, w_uv, w_o):
    lane = lax.broadcasted_iota(jnp.int32, (tok, wide - width), 1)
    penalty = jnp.where((lane == doc_ids[:, None]) | (lane == 4), -big, 0.0).astype(jnp.bfloat16)
    q = jnp.concatenate(
        [queries, jnp.broadcast_to(penalty[:, None, :], (tok, heads, wide - width))], axis=2
    )
    q = q.transpose(1, 0, 2).reshape(heads * tok, wide)
    ctx = lax.axis_index("ctx")
    info = jnp.stack([ctx % 2, ctx]).astype(jnp.int32)
    own, received, mates, q, info = gather(latent_kv, doc_ids, q, info)
    parts = attention(info, q, own, received, mates, w_uv, w_o)
    parts = lax.all_to_all(parts, "head", 0, 0)
    return jnp.sum(parts.astype(jnp.float32), axis=0).astype(jnp.bfloat16)


def solution(mesh):
    return jax.shard_map(
        local,
        mesh=mesh,
        in_specs=(
            P("ctx", "head", None),
            P("ctx", None),
            P("ctx"),
            P("head", None, None),
            P("head", None),
        ),
        out_specs=P("ctx", "head"),
        check_vma=False,
    )
```

```python
import functools

import jax
import jax.numpy as jnp
from jax import lax
from jax.experimental import pallas as pl
from jax.experimental.pallas import tpu as pltpu
from jax.sharding import PartitionSpec as P

score_scale = 0.07216878
log2e = 1.4426950408889634
tok, heads, width, latent, vdim = 192, 16, 576, 512, 128
wide = 640
back = 8
window = 1792
own_at = back * tok
group = 2 * tok
groups = heads * tok // group
big = 2.0**100
peers = 8
columns = 512


def attend(
    info, q_hbm, own, r1, r2, r3, r4, m0, m1, m2, m3, m4, wuv_hbm, wo_hbm, out, *rest
):
    keys, q, wuv, wo, s_a, s_b, p_a, p_b, bias, lat, ho, made, q_sem, w_sem, wo_sem, out_sem = rest
    core, ctx = info[0], info[1]

    def q_copy(i):
        return pltpu.make_async_copy(
            q_hbm.at[pl.ds(i * group, group)], q.at[pl.ds(i * group, group)], q_sem.at[i]
        )

    def wo_copy(k):
        return pltpu.make_async_copy(wo_hbm.at[:, pl.ds(pl.multiple_of(k * columns, columns), columns)], wo.at[k], wo_sem.at[k])

    q_copy(0).start()
    wuv_copy = pltpu.make_async_copy(wuv_hbm, wuv, w_sem)

    keys[pl.ds(9 * tok, window - 9 * tok), :] = jnp.zeros((window - 9 * tok, wide), jnp.bfloat16)
    bias[...] = jnp.where(
        lax.broadcasted_iota(jnp.int32, (tok, 256), 1) <= lax.broadcasted_iota(jnp.int32, (tok, 256), 0),
        0.0,
        -big,
    )
    q_copy(0).wait()
    for i in range(1, groups):
        q_copy(i).start()
    wuv_copy.start()
    for k in range(peers):
        wo_copy(k).start()
    missing = (lax.broadcasted_iota(jnp.int32, (tok, 128), 1) == width + 4 - latent).astype(jnp.bfloat16)
    odd = ((m4, m3), (m3, m2), (m2, m1), (m1, m0))
    even = (r4, r3, r2, r1)
    for block in range(back):
        at = slice(block * tok, (block + 1) * tok)
        if block % 2:
            pair = odd[block // 2]
            keys[at, :latent] = jnp.where(core == 0, pair[0][:, :latent], pair[1][:, :latent])
            tail = jnp.where(core == 0, pair[0][:, latent:], pair[1][:, latent:])
        else:
            keys[at, :latent] = even[block // 2][:, :latent]
            tail = even[block // 2][:, latent:]
        keys[at, latent:] = jnp.where(ctx + block < back, missing, tail)
    keys[own_at : own_at + tok, :] = own[...]

    def scores(i, s):
        rows = q[pl.ds(pl.multiple_of(i * group, group), group), :]
        for j in range(window // 256):
            part = lax.dot_general(
                rows,
                keys[j * 256 : (j + 1) * 256, :],
                (((1,), (1,)), ((), ())),
                preferred_element_type=jnp.float32,
            )
            if j == own_at // 256:
                part = part + jnp.concatenate([bias[...], bias[...]], axis=0)
            s[:, j * 256 : (j + 1) * 256] = part

    def finish(i, s, p):
        top = jnp.max(s[...], axis=1, keepdims=True)
        total = jnp.zeros((group, 1), jnp.float32)
        for j in range(window // 256):
            e = jnp.exp2((s[:, j * 256 : (j + 1) * 256] - top) * (score_scale * log2e))
            total = total + jnp.sum(e, axis=1, keepdims=True)
            p[:, j * 256 : (j + 1) * 256] = e.astype(jnp.bfloat16)
        acc = jnp.dot(p[...], keys[:, :latent], preferred_element_type=jnp.float32)
        lat[pl.ds(pl.multiple_of(i * group, group), group), :] = (acc / total).astype(jnp.bfloat16)

    scores(0, s_a)

    @pl.loop(0, groups // 2 - 1)
    def _(n):
        i = 2 * n
        q_copy(i + 1).wait()
        q_copy(i + 2).wait()
        scores(i + 1, s_b)
        finish(i, s_a, p_a)
        scores(i + 2, s_a)
        finish(i + 1, s_b, p_b)

    q_copy(groups - 1).wait()
    scores(groups - 1, s_b)
    finish(groups - 2, s_a, p_a)
    finish(groups - 1, s_b, p_b)

    wuv_copy.wait()

    @pl.loop(0, heads // 4)
    def _(n):
        for u in range(4):
            h = 4 * n + u
            ho[:, pl.ds(pl.multiple_of(h * vdim, vdim), vdim)] = jnp.dot(
                lat[pl.ds(pl.multiple_of(h * tok, tok), tok), :], wuv[h], preferred_element_type=jnp.float32
            ).astype(jnp.bfloat16)

    def out_copy(k):
        return pltpu.make_async_copy(made.at[k], out.at[k], out_sem.at[k])

    @pl.loop(0, peers // 2)
    def _(n):
        wo_copy(2 * n).wait()
        wo_copy(2 * n + 1).wait()
        for u in range(2):
            k = 2 * n + u
            made[k] = jnp.dot(ho[...], wo[k], preferred_element_type=jnp.float32).astype(jnp.bfloat16)
            out_copy(k).start()

    for k in range(peers):
        out_copy(k).wait()


def attention(info, q, own, received, mates, w_uv, w_o):
    hbm = pl.BlockSpec(memory_space=pl.ANY)
    vmem = pl.BlockSpec(memory_space=pltpu.VMEM)
    return pl.pallas_call(
        attend,
        out_shape=jax.ShapeDtypeStruct((peers, tok, columns), jnp.bfloat16),
        in_specs=[pl.BlockSpec(memory_space=pltpu.SMEM), hbm] + [vmem] * 10 + [hbm] * 2,
        out_specs=hbm,
        scratch_shapes=[
            pltpu.VMEM((window, wide), jnp.bfloat16),
            pltpu.VMEM((heads * tok, wide), jnp.bfloat16),
            pltpu.VMEM((heads, latent, vdim), jnp.bfloat16),
            pltpu.VMEM((peers, heads * vdim, columns), jnp.bfloat16),
            pltpu.VMEM((group, window), jnp.float32),
            pltpu.VMEM((group, window), jnp.float32),
            pltpu.VMEM((group, window), jnp.bfloat16),
            pltpu.VMEM((group, window), jnp.bfloat16),
            pltpu.VMEM((tok, 256), jnp.float32),
            pltpu.VMEM((heads * tok, latent), jnp.bfloat16),
            pltpu.VMEM((tok, heads * vdim), jnp.bfloat16),
            pltpu.VMEM((peers, tok, columns), jnp.bfloat16),
            pltpu.SemaphoreType.DMA((groups,)),
            pltpu.SemaphoreType.DMA,
            pltpu.SemaphoreType.DMA((peers,)),
            pltpu.SemaphoreType.DMA((peers,)),
        ],
        compiler_params=pltpu.CompilerParams(vmem_limit_bytes=50 * 1024 * 1024),
        cost_estimate=pl.CostEstimate(
            flops=24_000_000_000, bytes_accessed=26_000_000, transcendentals=5_500_000
        ),
        name="attend",
    )(info, q, own, *received, *mates, w_uv, w_o)


def extend(block, docs):
    lane = lax.broadcasted_iota(jnp.int32, (tok, wide), 1) - width
    other = (lane >= 0) & (lane < 4) & (lane != docs.astype(jnp.int32)[:, None])
    return jnp.where(other, 1.0, jnp.pad(block, ((0, 0), (0, wide - width)))).astype(jnp.bfloat16)


def gather(latent_kv, doc_ids, q, info):
    ctx = lax.axis_index("ctx")
    y = (ctx // 2) % 4
    swap = functools.partial(lax.ppermute, axis_name="ctx", perm=[(i, i ^ 1) for i in range(16)])
    cross = functools.partial(
        lax.ppermute,
        axis_name=("ctx", "head"),
        perm=[(c * 8 + h, (c + 8) * 8 + (h ^ 1)) for c in range(8) for h in range(8)],
    )
    docs = doc_ids.astype(jnp.bfloat16)
    moved, moved_docs = cross(latent_kv), cross(docs)
    own, moved = lax.optimization_barrier((extend(latent_kv, docs), moved))
    crossed = extend(moved, moved_docs)
    later, later_docs = lax.optimization_barrier((moved, moved_docs))
    received = {}
    for k in (2, 1, 3):
        perm = [(i, (i // 8) * 8 + (i % 8 + 2 * k) % 8) for i in range(16)]
        received[k] = lax.ppermute(jnp.where(y + k < 4, own, crossed), "ctx", perm)
    received[1], q, info = lax.optimization_barrier((received[1], q, info))
    received = [received[1], received[2], received[3], extend(later, later_docs)]
    mates = [swap(block) for block in [own] + received]
    return own, received, mates, q, info


def local(queries, latent_kv, doc_ids, w_uv, w_o):
    lane = lax.broadcasted_iota(jnp.int32, (tok, wide - width), 1)
    penalty = jnp.where((lane == doc_ids[:, None]) | (lane == 4), -big, 0.0).astype(jnp.bfloat16)
    q = jnp.concatenate(
        [queries, jnp.broadcast_to(penalty[:, None, :], (tok, heads, wide - width))], axis=2
    )
    q = q.transpose(1, 0, 2).reshape(heads * tok, wide)
    ctx = lax.axis_index("ctx")
    info = jnp.stack([ctx % 2, ctx]).astype(jnp.int32)
    own, received, mates, q, info = gather(latent_kv, doc_ids, q, info)
    parts = attention(info, q, own, received, mates, w_uv, w_o)
    parts = lax.all_to_all(parts, "head", 0, 0)
    return jnp.sum(parts.astype(jnp.float32), axis=0).astype(jnp.bfloat16)


def solution(mesh):
    return jax.shard_map(
        local,
        mesh=mesh,
        in_specs=(
            P("ctx", "head", None),
            P("ctx", None),
            P("ctx"),
            P("head", None, None),
            P("head", None),
        ),
        out_specs=P("ctx", "head"),
        check_vma=False,
    )
```

```python
import functools

import jax
import jax.numpy as jnp
from jax import lax
from jax.experimental import pallas as pl
from jax.experimental.pallas import tpu as pltpu
from jax.sharding import PartitionSpec as P

score_scale = 0.07216878
log2e = 1.4426950408889634
tok, heads, width, latent, vdim = 192, 16, 576, 512, 128
wide = 640
back = 8
window = 1792
own_at = back * tok
group = 2 * tok
groups = heads * tok // group
big = 2.0**100
peers = 8
columns = 512


def attend(
    q_hbm, own, r1, r2, r3, r4, m0, m1, m2, m3, m4, wuv_hbm, wo_hbm, out, *rest
):
    keys, q, wuv, wo, s_a, s_b, p_a, p_b, bias, lat, ho, made, q_sem, w_sem, wo_sem, out_sem = rest
    ctx = lax.axis_index("ctx")
    core = lax.rem(ctx, 2)

    def q_copy(i):
        return pltpu.make_async_copy(
            q_hbm.at[pl.ds(i * group, group)], q.at[pl.ds(i * group, group)], q_sem.at[i]
        )

    def wo_copy(k):
        return pltpu.make_async_copy(wo_hbm.at[:, pl.ds(pl.multiple_of(k * columns, columns), columns)], wo.at[k], wo_sem.at[k])

    q_copy(0).start()
    wuv_copy = pltpu.make_async_copy(wuv_hbm, wuv, w_sem)

    keys[pl.ds(9 * tok, window - 9 * tok), :] = jnp.zeros((window - 9 * tok, wide), jnp.bfloat16)
    bias[...] = jnp.where(
        lax.broadcasted_iota(jnp.int32, (tok, 256), 1) <= lax.broadcasted_iota(jnp.int32, (tok, 256), 0),
        0.0,
        -big,
    )
    q_copy(0).wait()
    for i in range(1, groups):
        q_copy(i).start()
    wuv_copy.start()
    for k in range(peers):
        wo_copy(k).start()
    missing = (lax.broadcasted_iota(jnp.int32, (tok, 128), 1) == width + 4 - latent).astype(jnp.bfloat16)
    odd = ((m4, m3), (m3, m2), (m2, m1), (m1, m0))
    even = (r4, r3, r2, r1)
    for block in range(back):
        at = slice(block * tok, (block + 1) * tok)
        if block % 2:
            pair = odd[block // 2]
            keys[at, :latent] = jnp.where(core == 0, pair[0][:, :latent], pair[1][:, :latent])
            tail = jnp.where(core == 0, pair[0][:, latent:], pair[1][:, latent:])
        else:
            keys[at, :latent] = even[block // 2][:, :latent]
            tail = even[block // 2][:, latent:]
        keys[at, latent:] = jnp.where(ctx + block < back, missing, tail)
    keys[own_at : own_at + tok, :] = own[...]

    def scores(i, s):
        rows = q[pl.ds(pl.multiple_of(i * group, group), group), :]
        for j in range(window // 256):
            part = lax.dot_general(
                rows,
                keys[j * 256 : (j + 1) * 256, :],
                (((1,), (1,)), ((), ())),
                preferred_element_type=jnp.float32,
            )
            if j == own_at // 256:
                part = part + jnp.concatenate([bias[...], bias[...]], axis=0)
            s[:, j * 256 : (j + 1) * 256] = part

    def finish(i, s, p):
        top = jnp.max(s[...], axis=1, keepdims=True)
        total = jnp.zeros((group, 1), jnp.float32)
        for j in range(window // 256):
            e = jnp.exp2((s[:, j * 256 : (j + 1) * 256] - top) * (score_scale * log2e))
            total = total + jnp.sum(e, axis=1, keepdims=True)
            p[:, j * 256 : (j + 1) * 256] = e.astype(jnp.bfloat16)
        acc = jnp.dot(p[...], keys[:, :latent], preferred_element_type=jnp.float32)
        lat[pl.ds(pl.multiple_of(i * group, group), group), :] = (acc / total).astype(jnp.bfloat16)

    scores(0, s_a)

    @pl.loop(0, groups // 2 - 1)
    def _(n):
        i = 2 * n
        q_copy(i + 1).wait()
        q_copy(i + 2).wait()
        scores(i + 1, s_b)
        finish(i, s_a, p_a)
        scores(i + 2, s_a)
        finish(i + 1, s_b, p_b)

    q_copy(groups - 1).wait()
    scores(groups - 1, s_b)
    finish(groups - 2, s_a, p_a)
    finish(groups - 1, s_b, p_b)

    wuv_copy.wait()

    @pl.loop(0, heads // 4)
    def _(n):
        for u in range(4):
            h = 4 * n + u
            ho[:, pl.ds(pl.multiple_of(h * vdim, vdim), vdim)] = jnp.dot(
                lat[pl.ds(pl.multiple_of(h * tok, tok), tok), :], wuv[h], preferred_element_type=jnp.float32
            ).astype(jnp.bfloat16)

    def out_copy(k):
        return pltpu.make_async_copy(made.at[k], out.at[k], out_sem.at[k])

    @pl.loop(0, peers // 2)
    def _(n):
        wo_copy(2 * n).wait()
        wo_copy(2 * n + 1).wait()
        for u in range(2):
            k = 2 * n + u
            made[k] = jnp.dot(ho[...], wo[k], preferred_element_type=jnp.float32).astype(jnp.bfloat16)
            out_copy(k).start()

    for k in range(peers):
        out_copy(k).wait()


def attention(q, own, received, mates, w_uv, w_o):
    hbm = pl.BlockSpec(memory_space=pl.ANY)
    vmem = pl.BlockSpec(memory_space=pltpu.VMEM)
    return pl.pallas_call(
        attend,
        out_shape=jax.ShapeDtypeStruct((peers, tok, columns), jnp.bfloat16),
        in_specs=[hbm] + [vmem] * 10 + [hbm] * 2,
        out_specs=hbm,
        scratch_shapes=[
            pltpu.VMEM((window, wide), jnp.bfloat16),
            pltpu.VMEM((heads * tok, wide), jnp.bfloat16),
            pltpu.VMEM((heads, latent, vdim), jnp.bfloat16),
            pltpu.VMEM((peers, heads * vdim, columns), jnp.bfloat16),
            pltpu.VMEM((group, window), jnp.float32),
            pltpu.VMEM((group, window), jnp.float32),
            pltpu.VMEM((group, window), jnp.bfloat16),
            pltpu.VMEM((group, window), jnp.bfloat16),
            pltpu.VMEM((tok, 256), jnp.float32),
            pltpu.VMEM((heads * tok, latent), jnp.bfloat16),
            pltpu.VMEM((tok, heads * vdim), jnp.bfloat16),
            pltpu.VMEM((peers, tok, columns), jnp.bfloat16),
            pltpu.SemaphoreType.DMA((groups,)),
            pltpu.SemaphoreType.DMA,
            pltpu.SemaphoreType.DMA((peers,)),
            pltpu.SemaphoreType.DMA((peers,)),
        ],
        compiler_params=pltpu.CompilerParams(vmem_limit_bytes=50 * 1024 * 1024),
        cost_estimate=pl.CostEstimate(
            flops=24_000_000_000, bytes_accessed=26_000_000, transcendentals=5_500_000
        ),
        name="attend",
    )(q, own, *received, *mates, w_uv, w_o)


def extend(block, docs):
    lane = lax.broadcasted_iota(jnp.int32, (tok, wide), 1) - width
    other = (lane >= 0) & (lane < 4) & (lane != docs.astype(jnp.int32)[:, None])
    return jnp.where(other, 1.0, jnp.pad(block, ((0, 0), (0, wide - width)))).astype(jnp.bfloat16)


def gather(latent_kv, doc_ids, q):
    ctx = lax.axis_index("ctx")
    y = (ctx // 2) % 4
    swap = functools.partial(lax.ppermute, axis_name="ctx", perm=[(i, i ^ 1) for i in range(16)])
    cross = functools.partial(
        lax.ppermute,
        axis_name=("ctx", "head"),
        perm=[(c * 8 + h, (c + 8) * 8 + (h ^ 1)) for c in range(8) for h in range(8)],
    )
    docs = doc_ids.astype(jnp.bfloat16)
    moved, moved_docs = cross(latent_kv), cross(docs)
    own, moved = lax.optimization_barrier((extend(latent_kv, docs), moved))
    crossed = extend(moved, moved_docs)
    later, later_docs = lax.optimization_barrier((moved, moved_docs))
    received = {}
    for k in (2, 1, 3):
        perm = [(i, (i // 8) * 8 + (i % 8 + 2 * k) % 8) for i in range(16)]
        received[k] = lax.ppermute(jnp.where(y + k < 4, own, crossed), "ctx", perm)
    received[1], q = lax.optimization_barrier((received[1], q))
    received = [received[1], received[2], received[3], extend(later, later_docs)]
    mates = [swap(block) for block in [own] + received]
    return own, received, mates, q


def local(queries, latent_kv, doc_ids, w_uv, w_o):
    lane = lax.broadcasted_iota(jnp.int32, (tok, wide - width), 1)
    penalty = jnp.where((lane == doc_ids[:, None]) | (lane == 4), -big, 0.0).astype(jnp.bfloat16)
    q = jnp.concatenate(
        [queries, jnp.broadcast_to(penalty[:, None, :], (tok, heads, wide - width))], axis=2
    )
    q = q.transpose(1, 0, 2).reshape(heads * tok, wide)
    own, received, mates, q = gather(latent_kv, doc_ids, q)
    parts = attention(q, own, received, mates, w_uv, w_o)
    parts = lax.all_to_all(parts, "head", 0, 0)
    return jnp.sum(parts.astype(jnp.float32), axis=0).astype(jnp.bfloat16)


def solution(mesh):
    return jax.shard_map(
        local,
        mesh=mesh,
        in_specs=(
            P("ctx", "head", None),
            P("ctx", None),
            P("ctx"),
            P("head", None, None),
            P("head", None),
        ),
        out_specs=P("ctx", "head"),
        check_vma=False,
    )
```
